32 devices in a mesh: grp: 2 (over y), blk: 4 (over z), feat: 4 (over x, core).
Axes of the slice: x: 2, y: 2, z: 4, core: 2. Of those that a mesh axis runs over, the one named last changes fastest.
Arguments:
- queries: bfloat16 [512, 4096], P(('grp', 'blk'), 'feat'), parts along dimension 0, may hold values from -6 to 6
- inv_gram: bfloat16 [4096, 4096], P('feat', 'blk'), may hold values from -0.09375 to 0.09375
- store: bfloat16 [4096, 4096], P(('grp', 'blk'), 'feat'), parts along dimension 0, may hold values from -0.09375 to 0.09375
- example_ids: int32 [2048], P(('grp', 'blk')), parts along dimension 0, may hold values from 0 to 511
- example_weights: float32 [2048], P(('grp', 'blk')), parts along dimension 0, may hold values from 0.2 to 1
- domain_mask: int32 [8, 4], P('grp', 'blk'), parts along dimension 0, may hold values from 0 to 1, as said below
Outputs:
- scores: float32 [4, 128, 1024], P(None, ('grp', 'feat'), 'blk'), parts along dimension 1
The draws below stay inside these ranges and needn't reach their ends.
There are 2 independent parts, one for each index of `grp`. The reference program is written for one: setup_inputs(seed, part) draws one part's arguments, and reference() takes and returns one part's arrays. A program takes and returns all parts, laid end to end along the dimension named above; an argument that names none is the same for every part. Nothing has to cross between parts.
Inputs may be any that keep to these rules, and one draw needn't show every extreme that they name: `domain_mask`: each example block is scored against at least one query block.
All inputs are finite; a program needn't handle non-finite values.
Results may differ from the reference program's by a relative error of at most 0.015.
Values may be sent and summed in bfloat16 or wider, within the bound.
A program may use at most 64 MiB of HBM per device.

```python
import math
import jax
import jax.numpy as jnp
from jax import lax

PROJ = 4096
QDEV = 64
EDEV = 256
STORE = 512
QUERIES = 256
EXAMPLES = 1024
FBLK = 1024
N_BLK = 4
N_FEAT = 4


def draw_domain_mask(key, part):
    key = jax.random.fold_in(key, 7)
    key_heavy, key_forced, key_order = jax.random.split(key, 3)
    heavy = jax.random.randint(key_heavy, (N_BLK,), 0, 6) == 0
    forced = jax.random.randint(key_forced, (), 0, N_BLK)
    heavy = heavy | (jnp.arange(N_BLK) == forced)
    counts = jnp.where(heavy, max(1, 3 * N_BLK // 4), max(1, N_BLK // 4))
    noise = jax.random.randint(key_order, (N_BLK, N_BLK), 0, 1000)
    ranked = noise * N_BLK + jnp.arange(N_BLK)[:, None]
    ranks = jnp.argsort(jnp.argsort(ranked, axis=0), axis=0)
    return (ranks < counts[None, :]).astype(jnp.int32)


def with_ends(result, key, low, high):
    longest = result.shape.index(max(result.shape))
    spots = []
    for shift in (0, 1):
        where = [jax.random.randint(jax.random.fold_in(key, axis), (), 0, length) for axis, length in enumerate(result.shape)]
        where[longest] = (where[longest] + shift) % result.shape[longest]
        spots.append(tuple(where))
    return result.at[spots[0]].set(low).at[spots[1]].set(high)


def steps_of(own_key, shape, shards, smallest, largest):
    gain, own = 1.0, jax.random.fold_in(own_key, 6)
    for dim, parts in shards:
        steps = jnp.exp(jax.random.uniform(jax.random.fold_in(own, dim), (parts,), jnp.float32, smallest / len(shards), largest / len(shards)))
        gain = gain * jnp.repeat(steps, shape[dim] // parts).reshape([-1 if axis == dim else 1 for axis in range(len(shape))])
    return gain


def scatter_about(own_key, extent, scale, most, shards=(), held_as=jnp.bfloat16):
    drawn = jax.random.normal(own_key, extent, jnp.float32) * scale
    if len(shards) > 0:
        drawn = steps_of(own_key, extent, shards, -0.22, 0.18) * drawn
    return jnp.clip(drawn, min=-most, max=most).astype(held_as)


def setup_inputs(seed: int = 0, part: int = 0) -> dict:
    arg_keys = jax.random.split(jax.random.key(seed), 7)
    part_keys = jax.random.split(jax.random.fold_in(arg_keys[6], part), 7)
    queries = scatter_about(part_keys[0], (QUERIES, PROJ), 1.0, 6.0, ((0, 4), (1, 4)))
    inv_gram = scatter_about(arg_keys[1], (PROJ, PROJ), PROJ ** -0.5, 0.09375, ((0, 4), (1, 4)))
    store = scatter_about(part_keys[2], (STORE * N_BLK, PROJ), PROJ ** -0.5, 0.09375, ((0, 4), (1, 4)))
    example_ids = with_ends(jax.random.randint(part_keys[3], (EXAMPLES,), 0, STORE), jax.random.fold_in(part_keys[3], 1), 0, STORE - 1).astype(jnp.int32)
    example_weights = jnp.clip(jnp.exp(math.log(1.0) - 1.609438 * jax.random.uniform(part_keys[4], (EXAMPLES,), jnp.float32) ** steps_of(part_keys[4], (EXAMPLES,), ((0, 4),), -0.2, 0.2)), 0.2, 1.0)
    domain_mask = draw_domain_mask(jax.random.fold_in(jax.random.fold_in(arg_keys[6], part), 71), part)
    return {"queries": queries, "inv_gram": inv_gram, "store": store, "example_ids": example_ids, "example_weights": example_weights, "domain_mask": domain_mask}


def contract(left, right):
    return lax.dot_general(left, right, (((1,), (1,)), ((), ())), preferred_element_type=jnp.float32)


def reference(queries, inv_gram, store, example_ids, example_weights, domain_mask):
    precond = jnp.dot(queries, inv_gram, preferred_element_type=jnp.float32).astype(jnp.bfloat16)
    rows = ((jnp.arange(N_BLK * EDEV) // EDEV) * STORE + example_ids).astype(jnp.int32)
    examples = jnp.take(store, rows, axis=0)
    total = jnp.zeros((N_BLK * QDEV, N_BLK * EDEV), jnp.float32)
    for group in range(N_FEAT):
        part = contract(precond[:, group * FBLK:(group + 1) * FBLK], examples[:, group * FBLK:(group + 1) * FBLK])
        part = lax.optimization_barrier(part.astype(jnp.bfloat16)).astype(jnp.float32)
        total = total + part
    raw = total.reshape(N_BLK, QDEV, N_BLK * EDEV)
    spread = jnp.repeat(domain_mask, EDEV, axis=1).astype(jnp.float32)
    return raw * spread[:, None, :] * example_weights[None, None, :]
```

```python
import functools

import jax
import jax.numpy as jnp
from jax import lax
from jax.experimental import pallas as pl
from jax.experimental.pallas import tpu as pltpu
from jax.sharding import PartitionSpec as P

MESH = pl.DeviceIdType.MESH


def contract(left, right):
    return lax.dot_general(
        left, right, (((1,), (1,)), ((), ())), preferred_element_type=jnp.float32
    )


def kernel(
    n_blk,
    n_feat,
    q_hbm,
    g_hbm,
    store_hbm,
    ids_ref,
    out_ref,
    q_all,
    gram,
    stored,
    e_all,
    p_send,
    p_recv,
    cond,
    local_sem,
    a_send,
    a_recv,
    e_send,
    e_recv,
    b_send,
    b_recv,
    c_send,
    c_recv,
):
    z = lax.axis_index("blk")
    f = lax.axis_index("feat")
    half = z // 2
    order = [z, 1 + 4 * half - z, 2 - half, 3 - 3 * half]
    sibling = f + 1 - 2 * (f % 2)
    across = (f + 2) % 4

    load_q = pltpu.make_async_copy(q_hbm, q_all.at[z], local_sem.at[0])
    load_g = pltpu.make_async_copy(g_hbm, gram, local_sem.at[1])
    load_s = pltpu.make_async_copy(store_hbm, stored, local_sem.at[2])
    load_q.start()
    load_g.start()
    load_s.start()

    def send(src, dst, send_sem, recv_sem, target):
        return pltpu.make_async_remote_copy(
            src_ref=src,
            dst_ref=dst,
            send_sem=send_sem,
            recv_sem=recv_sem,
            device_id=target,
            device_id_type=MESH,
        )

    barrier = pltpu.get_barrier_semaphore()
    for d in range(1, n_blk):
        pl.semaphore_signal(
            barrier, inc=1, device_id={"blk": (z + d) % n_blk}, device_id_type=MESH
        )
    for d in range(1, n_feat):
        pl.semaphore_signal(
            barrier, inc=1, device_id={"feat": (f + d) % n_feat}, device_id_type=MESH
        )
    pl.semaphore_wait(barrier, n_blk + n_feat - 2)

    def a_copy(j, target):
        return send(
            q_all.at[j], q_all.at[j], a_send.at[target], a_recv.at[j], {"blk": target}
        )

    def b_copy(j, src, target):
        return send(
            p_send.at[j, target],
            p_recv.at[j, src],
            b_send.at[j, target],
            b_recv.at[j, src],
            {"feat": target},
        )

    def c_copy(c, j, target):
        return send(
            cond.at[c, j],
            cond.at[c, j],
            c_send.at[j, target],
            c_recv.at[c, j],
            {"blk": target},
        )

    def e_copy(src, slot, target):
        return send(
            e_all.at[src], e_all.at[src], e_send.at[slot], e_recv.at[src], {"feat": target}
        )

    load_q.wait()
    for s in range(1, n_blk):
        a_copy(z, order[s]).start()

    def multiply(s):
        j = order[s]
        if s > 0:
            a_copy(j, z).wait_recv()
        value = jnp.dot(q_all[j], gram[...], preferred_element_type=jnp.float32)
        rows = value.shape[0] // n_feat
        p_send[j] = value.astype(jnp.bfloat16).reshape(n_feat, rows, value.shape[1])
        for d in range(1, n_feat):
            b_copy(j, f, (f + d) % n_feat).start()

    def finish(s):
        j = order[s]
        total = p_send[j, f].astype(jnp.float32)
        for d in range(1, n_feat):
            src = (f + d) % n_feat
            b_copy(j, src, f).wait_recv()
            total = total + p_recv[j, src].astype(jnp.float32)
        cond[z, j] = total.astype(jnp.bfloat16)
        for t in range(1, n_blk):
            c_copy(z, j, order[t]).start()

    load_g.wait()
    multiply(0)

    load_s.wait()
    held = stored.shape[0]
    examples = ids_ref.shape[1]
    pick = jnp.where(
        lax.broadcasted_iota(jnp.int32, (held, examples), 0) == ids_ref[...], 1.0, 0.0
    ).astype(jnp.bfloat16)
    e_all[f] = lax.dot_general(
        pick, stored[...], (((0,), (0,)), ((), ())), preferred_element_type=jnp.float32
    ).astype(jnp.bfloat16)
    e_copy(f, 0, across).start()
    e_copy(f, 1, sibling).start()

    finish(0)
    multiply(1)
    finish(1)
    multiply(2)
    finish(2)
    multiply(3)
    e_copy(across, 2, f).wait_recv()
    e_copy(across, 2, sibling).start()
    finish(3)
    e_copy(sibling, 1, f).wait_recv()
    e_copy((sibling + 2) % 4, 1, f).wait_recv()

    total = None
    for s in range(n_blk):
        c = order[s]
        if s > 0:
            for t in range(n_blk):
                c_copy(c, order[t], z).wait_recv()
        rows = cond.shape[1] * cond.shape[2]
        value = contract(cond[c].reshape(rows, cond.shape[3]), e_all[c])
        total = value if total is None else total + value
    out_ref[...] = total.reshape(out_ref.shape)

    for s in range(1, n_blk):
        a_copy(z, order[s]).wait_send()
    for j in range(n_blk):
        for d in range(1, n_feat):
            b_copy(j, f, (f + d) % n_feat).wait_send()
        for s in range(1, n_blk):
            c_copy(z, j, order[s]).wait_send()
    for slot in range(3):
        e_copy(f, slot, sibling).wait_send()


def fused(n_blk, n_feat, queries, inv_gram, store, ids):
    qdev, width = queries.shape
    edev = ids.shape[1]
    rows = qdev // n_feat
    dma = pltpu.SemaphoreType.DMA
    any_spec = pl.BlockSpec(memory_space=pl.ANY)
    vmem_spec = pl.BlockSpec(memory_space=pltpu.VMEM)
    return pl.pallas_call(
        functools.partial(kernel, n_blk, n_feat),
        out_shape=jax.ShapeDtypeStruct((n_blk, rows, edev), jnp.float32),
        in_specs=[any_spec, any_spec, any_spec, vmem_spec],
        out_specs=vmem_spec,
        scratch_shapes=[
            pltpu.VMEM((n_blk, qdev, width), jnp.bfloat16),
            pltpu.VMEM(inv_gram.shape, jnp.bfloat16),
            pltpu.VMEM(store.shape, jnp.bfloat16),
            pltpu.VMEM((n_feat, edev, width), jnp.bfloat16),
            pltpu.VMEM((n_blk, n_feat, rows, inv_gram.shape[1]), jnp.bfloat16),
            pltpu.VMEM((n_blk, n_feat, rows, inv_gram.shape[1]), jnp.bfloat16),
            pltpu.VMEM((n_blk, n_blk, rows, inv_gram.shape[1]), jnp.bfloat16),
            dma((3,)),
            dma((n_blk,)),
            dma((n_blk,)),
            dma((3,)),
            dma((n_feat,)),
            dma((n_blk, n_feat)),
            dma((n_blk, n_feat)),
            dma((n_blk, n_blk)),
            dma((n_blk, n_blk)),
        ],
        compiler_params=pltpu.CompilerParams(
            collective_id=0, has_side_effects=True, vmem_limit_bytes=40 * 1024 * 1024
        ),
    )(queries, inv_gram, store, ids)


def plain(n_blk, n_feat, queries, inv_gram, store, ids):
    gathered = lax.all_gather(queries, "blk", axis=0, tiled=True)
    partial_value = jnp.dot(gathered, inv_gram, preferred_element_type=jnp.float32)
    rows = queries.shape[0] // n_feat
    spread = partial_value.astype(jnp.bfloat16).reshape(n_blk, n_feat, rows, -1)
    precond = lax.psum_scatter(spread, "feat", scatter_dimension=1, tiled=True)
    precond = lax.all_gather(
        precond.reshape(n_blk * rows, -1), "blk", axis=1, tiled=True
    )
    examples = lax.all_gather(
        jnp.take(store, ids[0], axis=0), "feat", axis=1, tiled=True
    )
    return contract(precond, examples).reshape(n_blk, rows, -1)


def per_device(queries, inv_gram, store, example_ids, example_weights, domain_mask):
    n_blk, n_feat = lax.axis_size("blk"), lax.axis_size("feat")
    lines = n_blk == 4 and n_feat == 4
    aligned = queries.shape[0] % (16 * n_feat) == 0 and queries.shape[1] % 128 == 0
    same = queries.shape[1] == inv_gram.shape[1]
    score = fused if lines and aligned and same else plain
    raw = score(n_blk, n_feat, queries, inv_gram, store, example_ids[None, :])
    factor = domain_mask[:, :, None].astype(jnp.float32)
    return raw * factor * example_weights[None, None, :]


def solution(mesh):
    in_specs = (
        P(("grp", "blk"), "feat"),
        P("feat", "blk"),
        P(("grp", "blk"), "feat"),
        P(("grp", "blk")),
        P(("grp", "blk")),
        P("grp", "blk"),
    )
    out_specs = P(None, ("grp", "feat"), "blk")
    return jax.shard_map(
        per_device, mesh=mesh, in_specs=in_specs, out_specs=out_specs, check_vma=False
    )
```

```python
import functools

import jax
import jax.numpy as jnp
from jax import lax
from jax.experimental import pallas as pl
from jax.experimental.pallas import tpu as pltpu
from jax.sharding import PartitionSpec as P

MESH = pl.DeviceIdType.MESH
VMEM = 63 * 1024 * 1024


def contract(left, right):
    return lax.dot_general(
        left, right, (((1,), (1,)), ((), ())), preferred_element_type=jnp.float32
    )


def kernel(
    n_blk,
    n_feat,
    q_hbm,
    g_hbm,
    store_hbm,
    ids_hbm,
    mask_hbm,
    out_ref,
    ids_ref,
    mask_ref,
    q_all,
    gram,
    stored,
    e_all,
    p_send,
    p_recv,
    cond,
    local_sem,
    a_send,
    a_recv,
    e_send,
    e_recv,
    b_send,
    b_recv,
    c_send,
    c_recv,
):
    z = lax.axis_index("blk")
    f = lax.axis_index("feat")
    half = z // 2
    order = [z, 1 + 4 * half - z, 2 - half, 3 - 3 * half]
    near, middle, far = order[1], order[2], order[3]
    between = (z - 1) * (z - 2) == 0
    sibling = f + 1 - 2 * (f % 2)
    across = (f + 2) % 4

    load_q = pltpu.make_async_copy(q_hbm, q_all.at[z], local_sem.at[0])
    load_g = pltpu.make_async_copy(g_hbm, gram, local_sem.at[1])
    load_s = pltpu.make_async_copy(store_hbm, stored, local_sem.at[2])
    load_ids = pltpu.make_async_copy(ids_hbm, ids_ref, local_sem.at[3])
    load_mask = pltpu.make_async_copy(mask_hbm, mask_ref, local_sem.at[4])

    def send(src, dst, send_sem, recv_sem, target):
        return pltpu.make_async_remote_copy(
            src_ref=src,
            dst_ref=dst,
            send_sem=send_sem,
            recv_sem=recv_sem,
            device_id=target,
            device_id_type=MESH,
        )

    barrier = pltpu.get_barrier_semaphore()
    for d in range(1, n_blk):
        pl.semaphore_signal(
            barrier, inc=1, device_id={"blk": (z + d) % n_blk}, device_id_type=MESH
        )
    for d in range(1, n_feat):
        pl.semaphore_signal(
            barrier, inc=1, device_id={"feat": (f + d) % n_feat}, device_id_type=MESH
        )
    load_q.start()
    load_g.start()
    load_ids.start()
    load_s.start()
    load_mask.start()

    def a_copy(j, target, slot, src=None):
        return send(
            q_all.at[j] if src is None else src,
            q_all.at[j],
            a_send.at[slot],
            a_recv.at[j],
            {"blk": target},
        )

    def b_copy(j, src, target):
        return send(
            p_send.at[j, target],
            p_recv.at[j, src],
            b_send.at[j, target],
            b_recv.at[j, src],
            {"feat": target},
        )

    def c_copy(c, j, target, slot):
        return send(
            cond.at[c, j],
            cond.at[c, j],
            c_send.at[j, slot],
            c_recv.at[c, j],
            {"blk": target},
        )

    def e_copy(src, slot, target):
        return send(
            e_all.at[src], e_all.at[src], e_send.at[slot], e_recv.at[src], {"feat": target}
        )

    def multiply(s):
        j = order[s]
        if s > 0:
            a_copy(j, z, 0).wait_recv()
        if s >= 2:
            @pl.when(between)
            def _():
                a_copy(j, near, s).start()

        value = jnp.dot(q_all[j], gram[...], preferred_element_type=jnp.float32)
        rows = value.shape[0] // n_feat
        p_send[j] = value.astype(jnp.bfloat16).reshape(n_feat, rows, value.shape[1])

    def spread(s):
        for d in range(1, n_feat):
            b_copy(order[s], f, (f + d) % n_feat).start()

    def finish(s):
        j = order[s]
        total = p_send[j, f].astype(jnp.float32)
        for d in range(1, n_feat):
            src = (f + d) % n_feat
            b_copy(j, src, f).wait_recv()
            total = total + p_recv[j, src].astype(jnp.float32)
        cond[z, j] = total.astype(jnp.bfloat16)
        c_copy(z, j, near, 0).start()
        c_copy(z, j, middle, 1).start()

        @pl.when(between)
        def _():
            c_copy(z, j, far, 2).start()

    def hand_on(t):
        j = 3 - 3 * half + t * (2 * half - 1)

        @pl.when(between)
        def _():
            c_copy(far, j, z, 0).wait_recv()
            c_copy(far, j, near, 3).start()


    pl.semaphore_wait(barrier, n_blk + n_feat - 2)
    a_copy(z, near, 0, q_hbm).start()

    @pl.when(between)
    def _():
        a_copy(z, middle, 1, q_hbm).start()

    load_q.wait()
    load_g.wait()
    multiply(0)
    spread(0)
    load_ids.wait()
    load_s.wait()
    held = stored.shape[0]
    examples = ids_ref.shape[1]
    pick = jnp.where(
        lax.broadcasted_iota(jnp.int32, (held, examples), 0) == ids_ref[...], 1.0, 0.0
    ).astype(jnp.bfloat16)
    e_all[f] = lax.dot_general(
        pick, stored[...], (((0,), (0,)), ((), ())), preferred_element_type=jnp.float32
    ).astype(jnp.bfloat16)
    e_copy(f, 0, across).start()
    e_copy(f, 1, sibling).start()

    @pl.when(jnp.logical_not(between))
    def _():
        a_copy(z, near, 0, q_hbm).wait_send()
        a_copy(z, middle, 1, q_hbm).start()

    finish(0)
    multiply(1)
    spread(1)
    finish(1)
    multiply(2)
    spread(2)
    hand_on(0)
    finish(2)
    multiply(3)
    spread(3)
    hand_on(1)
    finish(3)
    hand_on(2)
    hand_on(3)
    e_copy(across, 2, f).wait_recv()
    e_copy(across, 2, sibling).start()
    e_copy(sibling, 1, f).wait_recv()
    e_copy((sibling + 2) % 4, 1, f).wait_recv()

    total = None
    for s in range(n_blk):
        c = order[s]
        if 0 < s < 3:
            for j in range(n_blk):
                c_copy(c, j, z, 0).wait_recv()
        if s == 3:

            @pl.when(jnp.logical_not(between))
            def _():
                for j in range(n_blk):
                    c_copy(c, j, z, 0).wait_recv()

        rows = cond.shape[1] * cond.shape[2]
        value = contract(cond[c].reshape(rows, cond.shape[3]), e_all[c])
        total = value if total is None else total + value
    load_mask.wait()
    total = total.reshape(out_ref.shape)
    for j in range(n_blk):
        out_ref[j] = total[j] * mask_ref[0, j].astype(jnp.float32)

    for j in range(n_blk):
        for d in range(1, n_feat):
            b_copy(j, f, (f + d) % n_feat).wait_send()
        c_copy(z, j, near, 0).wait_send()
        c_copy(z, j, middle, 1).wait_send()

    @pl.when(between)
    def _():
        for slot in range(4):
            a_copy(z, near, slot).wait_send()
        for j in range(n_blk):
            c_copy(z, j, far, 2).wait_send()
            c_copy(far, j, near, 3).wait_send()

    @pl.when(jnp.logical_not(between))
    def _():
        a_copy(z, middle, 1).wait_send()

    for slot in range(3):
        e_copy(f, slot, sibling).wait_send()


def fused(n_blk, n_feat, queries, inv_gram, store, ids, mask):
    qdev, width = queries.shape
    edev = ids.shape[1]
    rows = qdev // n_feat
    dma = pltpu.SemaphoreType.DMA
    any_spec = pl.BlockSpec(memory_space=pl.ANY)
    vmem_spec = pl.BlockSpec(memory_space=pltpu.VMEM)
    return pl.pallas_call(
        functools.partial(kernel, n_blk, n_feat),
        out_shape=jax.ShapeDtypeStruct((n_blk, rows, edev), jnp.float32),
        in_specs=[any_spec] * 5,
        out_specs=vmem_spec,
        scratch_shapes=[
            pltpu.VMEM(ids.shape, jnp.int32),
            pltpu.SMEM(mask.shape, jnp.int32),
            pltpu.VMEM((n_blk, qdev, width), jnp.bfloat16),
            pltpu.VMEM(inv_gram.shape, jnp.bfloat16),
            pltpu.VMEM(store.shape, jnp.bfloat16),
            pltpu.VMEM((n_feat, edev, width), jnp.bfloat16),
            pltpu.VMEM((n_blk, n_feat, rows, inv_gram.shape[1]), jnp.bfloat16),
            pltpu.VMEM((n_blk, n_feat, rows, inv_gram.shape[1]), jnp.bfloat16),
            pltpu.VMEM((n_blk, n_blk, rows, inv_gram.shape[1]), jnp.bfloat16),
            dma((5,)),
            dma((n_blk,)),
            dma((n_blk,)),
            dma((3,)),
            dma((n_feat,)),
            dma((n_blk, n_feat)),
            dma((n_blk, n_feat)),
            dma((n_blk, n_blk)),
            dma((n_blk, n_blk)),
        ],
        compiler_params=pltpu.CompilerParams(
            collective_id=0, has_side_effects=True, vmem_limit_bytes=VMEM
        ),
    )(queries, inv_gram, store, ids, mask)


def plain(n_blk, n_feat, queries, inv_gram, store, ids, mask):
    gathered = lax.all_gather(queries, "blk", axis=0, tiled=True)
    partial_value = jnp.dot(gathered, inv_gram, preferred_element_type=jnp.float32)
    rows = queries.shape[0] // n_feat
    spread = partial_value.astype(jnp.bfloat16).reshape(n_blk, n_feat, rows, -1)
    precond = lax.psum_scatter(spread, "feat", scatter_dimension=1, tiled=True)
    precond = lax.all_gather(
        precond.reshape(n_blk * rows, -1), "blk", axis=1, tiled=True
    )
    examples = lax.all_gather(
        jnp.take(store, ids[0], axis=0), "feat", axis=1, tiled=True
    )
    raw = contract(precond, examples).reshape(n_blk, rows, -1)
    return raw * mask[0][:, None, None].astype(jnp.float32)


def per_device(queries, inv_gram, store, example_ids, example_weights, domain_mask):
    n_blk, n_feat = lax.axis_size("blk"), lax.axis_size("feat")
    lines = n_blk == 4 and n_feat == 4
    aligned = queries.shape[0] % (16 * n_feat) == 0 and queries.shape[1] % 128 == 0
    same = queries.shape[1] == inv_gram.shape[1]
    score = fused if lines and aligned and same else plain
    ids, mask = example_ids[None, :], domain_mask.reshape(1, n_blk)
    raw = score(n_blk, n_feat, queries, inv_gram, store, ids, mask)
    return raw * example_weights[None, None, :]


def solution(mesh):
    in_specs = (
        P(("grp", "blk"), "feat"),
        P("feat", "blk"),
        P(("grp", "blk"), "feat"),
        P(("grp", "blk")),
        P(("grp", "blk")),
        P("grp", "blk"),
    )
    out_specs = P(None, ("grp", "feat"), "blk")
    return jax.shard_map(
        per_device, mesh=mesh, in_specs=in_specs, out_specs=out_specs, check_vma=False
    )
```

```python
import functools

import jax
import jax.numpy as jnp
from jax import lax
from jax.experimental import pallas as pl
from jax.experimental.pallas import tpu as pltpu
from jax.sharding import PartitionSpec as P

MESH = pl.DeviceIdType.MESH
VMEM = 63 * 1024 * 1024
PARTS = 4


def contract(left, right):
    return lax.dot_general(
        left, right, (((1,), (1,)), ((), ())), preferred_element_type=jnp.float32
    )


def kernel(
    n_blk,
    n_feat,
    q_hbm,
    g_hbm,
    store_hbm,
    ids_hbm,
    mask_hbm,
    out_ref,
    ids_ref,
    mask_ref,
    q_all,
    gram,
    stored,
    e_all,
    p_send,
    p_recv,
    cond,
    local_sem,
    a_send,
    a_recv,
    e_send,
    e_recv,
    b_send,
    b_recv,
    c_send,
    c_recv,
):
    z = lax.axis_index("blk")
    f = lax.axis_index("feat")
    half = z // 2
    order = [z, z + 1 - 2 * half, 2 - 2 * z + 5 * half, 3 - 3 * half]
    first, second, far = order[1], order[2], order[3]
    end = 3 * half
    between = (z - 1) * (z - 2) == 0
    sibling = f + 1 - 2 * (f % 2)
    across = (f + 2) % 4

    load_q = pltpu.make_async_copy(q_hbm, q_all.at[z], local_sem.at[0])
    load_g = pltpu.make_async_copy(g_hbm, gram, local_sem.at[1])
    load_s = pltpu.make_async_copy(store_hbm, stored, local_sem.at[2])
    load_ids = pltpu.make_async_copy(ids_hbm, ids_ref, local_sem.at[3])
    load_mask = pltpu.make_async_copy(mask_hbm, mask_ref, local_sem.at[4])

    def send(src, dst, send_sem, recv_sem, target):
        return pltpu.make_async_remote_copy(
            src_ref=src,
            dst_ref=dst,
            send_sem=send_sem,
            recv_sem=recv_sem,
            device_id=target,
            device_id_type=MESH,
        )

    barrier = pltpu.get_barrier_semaphore()
    for d in range(1, n_blk):
        pl.semaphore_signal(
            barrier, inc=1, device_id={"blk": (z + d) % n_blk}, device_id_type=MESH
        )
    for d in range(1, n_feat):
        pl.semaphore_signal(
            barrier, inc=1, device_id={"feat": (f + d) % n_feat}, device_id_type=MESH
        )
    load_q.start()
    load_g.start()
    load_ids.start()
    load_s.start()
    load_mask.start()

    def a_copy(j, target, slot, src=None):
        return send(
            q_all.at[j] if src is None else src,
            q_all.at[j],
            a_send.at[slot],
            a_recv.at[j],
            {"blk": target},
        )

    def b_copy(j, src, target):
        return send(
            p_send.at[j, target],
            p_recv.at[j, src],
            b_send.at[j, target],
            b_recv.at[j, src],
            {"feat": target},
        )

    def c_copy(c, j, target, slot):
        return send(
            cond.at[c, j],
            cond.at[c, j],
            c_send.at[j, slot],
            c_recv.at[c, j],
            {"blk": target},
        )

    def e_copy(src, slot, i, target):
        size = e_all.shape[1] // PARTS
        part = e_all.at[src, pl.ds(i * size, size)]
        return send(
            part, part, e_send.at[slot, i], e_recv.at[src, i], {"feat": target}
        )

    def push_e(i):
        if i < PARTS:
            e_copy(f, 0, i, across).start()
            e_copy(f, 1, i, sibling).start()

    def multiply(s):
        j = order[s]
        if s > 0:
            a_copy(j, z, 0).wait_recv()
        if s % 2 == 1:
            @pl.when(between)
            def _():
                a_copy(j, end, 2 + s // 2).start()

        value = jnp.dot(q_all[j], gram[...], preferred_element_type=jnp.float32)
        rows = value.shape[0] // n_feat
        p_send[j] = value.astype(jnp.bfloat16).reshape(n_feat, rows, value.shape[1])

    def spread(s):
        for d in range(1, n_feat):
            b_copy(order[s], f, (f + d) % n_feat).start()

    def finish(s):
        j = order[s]
        total = p_send[j, f].astype(jnp.float32)
        for d in range(1, n_feat):
            src = (f + d) % n_feat
            b_copy(j, src, f).wait_recv()
            total = total + p_recv[j, src].astype(jnp.float32)
        cond[z, j] = total.astype(jnp.bfloat16)
        for t in (3, 2, 1):
            c_copy(z, j, order[t], t - 1).start()

    pl.semaphore_wait(barrier, n_blk + n_feat - 2)
    a_copy(z, first, 0, q_hbm).start()
    a_copy(z, second, 1, q_hbm).start()

    load_q.wait()
    load_g.wait()
    multiply(0)
    spread(0)
    load_ids.wait()
    load_s.wait()
    held = stored.shape[0]
    examples = ids_ref.shape[1]
    pick = jnp.where(
        lax.broadcasted_iota(jnp.int32, (held, examples), 0) == ids_ref[...], 1.0, 0.0
    ).astype(jnp.bfloat16)
    e_all[f] = lax.dot_general(
        pick, stored[...], (((0,), (0,)), ((), ())), preferred_element_type=jnp.float32
    ).astype(jnp.bfloat16)
    push_e(0)

    @pl.when(jnp.logical_not(between))
    def _():
        pass

    multiply(1)
    spread(1)
    push_e(1)
    finish(0)
    multiply(2)
    spread(2)
    push_e(2)
    finish(1)
    multiply(3)
    spread(3)
    push_e(3)
    finish(2)
    finish(3)
    for i in range(PARTS):
        e_copy(across, 2, i, f).wait_recv()
        e_copy(across, 2, i, sibling).start()
    for i in range(PARTS):
        e_copy(sibling, 1, i, f).wait_recv()
        e_copy((sibling + 2) % 4, 1, i, f).wait_recv()

    total = None
    for s in range(n_blk):
        c = order[s]
        if s > 0:
            for j in range(n_blk):
                c_copy(c, j, z, 0).wait_recv()
        rows = cond.shape[1] * cond.shape[2]
        value = contract(cond[c].reshape(rows, cond.shape[3]), e_all[c])
        total = value if total is None else total + value
    load_mask.wait()
    total = total.reshape(out_ref.shape)
    for j in range(n_blk):
        out_ref[j] = total[j] * mask_ref[0, j].astype(jnp.float32)

    for j in range(n_blk):
        for d in range(1, n_feat):
            b_copy(j, f, (f + d) % n_feat).wait_send()
        for t in range(1, n_blk):
            c_copy(z, j, order[t], t - 1).wait_send()
    a_copy(z, first, 0).wait_send()
    a_copy(z, second, 1).wait_send()

    @pl.when(between)
    def _():
        for slot in (2, 3):
            a_copy(z, end, slot).wait_send()

    for slot in range(3):
        for i in range(PARTS):
            e_copy(f, slot, i, sibling).wait_send()


def fused(n_blk, n_feat, queries, inv_gram, store, ids, mask):
    qdev, width = queries.shape
    edev = ids.shape[1]
    rows = qdev // n_feat
    dma = pltpu.SemaphoreType.DMA
    any_spec = pl.BlockSpec(memory_space=pl.ANY)
    vmem_spec = pl.BlockSpec(memory_space=pltpu.VMEM)
    return pl.pallas_call(
        functools.partial(kernel, n_blk, n_feat),
        out_shape=jax.ShapeDtypeStruct((n_blk, rows, edev), jnp.float32),
        in_specs=[any_spec] * 5,
        out_specs=vmem_spec,
        scratch_shapes=[
            pltpu.VMEM(ids.shape, jnp.int32),
            pltpu.SMEM(mask.shape, jnp.int32),
            pltpu.VMEM((n_blk, qdev, width), jnp.bfloat16),
            pltpu.VMEM(inv_gram.shape, jnp.bfloat16),
            pltpu.VMEM(store.shape, jnp.bfloat16),
            pltpu.VMEM((n_feat, edev, width), jnp.bfloat16),
            pltpu.VMEM((n_blk, n_feat, rows, inv_gram.shape[1]), jnp.bfloat16),
            pltpu.VMEM((n_blk, n_feat, rows, inv_gram.shape[1]), jnp.bfloat16),
            pltpu.VMEM((n_blk, n_blk, rows, inv_gram.shape[1]), jnp.bfloat16),
            dma((5,)),
            dma((n_blk,)),
            dma((n_blk,)),
            dma((3, PARTS)),
            dma((n_feat, PARTS)),
            dma((n_blk, n_feat)),
            dma((n_blk, n_feat)),
            dma((n_blk, n_blk)),
            dma((n_blk, n_blk)),
        ],
        compiler_params=pltpu.CompilerParams(
            collective_id=0, has_side_effects=True, vmem_limit_bytes=VMEM
        ),
    )(queries, inv_gram, store, ids, mask)


def plain(n_blk, n_feat, queries, inv_gram, store, ids, mask):
    gathered = lax.all_gather(queries, "blk", axis=0, tiled=True)
    partial_value = jnp.dot(gathered, inv_gram, preferred_element_type=jnp.float32)
    rows = queries.shape[0] // n_feat
    spread = partial_value.astype(jnp.bfloat16).reshape(n_blk, n_feat, rows, -1)
    precond = lax.psum_scatter(spread, "feat", scatter_dimension=1, tiled=True)
    precond = lax.all_gather(
        precond.reshape(n_blk * rows, -1), "blk", axis=1, tiled=True
    )
    examples = lax.all_gather(
        jnp.take(store, ids[0], axis=0), "feat", axis=1, tiled=True
    )
    raw = contract(precond, examples).reshape(n_blk, rows, -1)
    return raw * mask[0][:, None, None].astype(jnp.float32)


def per_device(queries, inv_gram, store, example_ids, example_weights, domain_mask):
    n_blk, n_feat = lax.axis_size("blk"), lax.axis_size("feat")
    lines = n_blk == 4 and n_feat == 4
    aligned = queries.shape[0] % (16 * n_feat) == 0 and queries.shape[1] % 128 == 0
    same = queries.shape[1] == inv_gram.shape[1]
    score = fused if lines and aligned and same else plain
    ids, mask = example_ids[None, :], domain_mask.reshape(1, n_blk)
    raw = score(n_blk, n_feat, queries, inv_gram, store, ids, mask)
    return raw * example_weights[None, None, :]


def solution(mesh):
    in_specs = (
        P(("grp", "blk"), "feat"),
        P("feat", "blk"),
        P(("grp", "blk"), "feat"),
        P(("grp", "blk")),
        P(("grp", "blk")),
        P("grp", "blk"),
    )
    out_specs = P(None, ("grp", "feat"), "blk")
    return jax.shard_map(
        per_device, mesh=mesh, in_specs=in_specs, out_specs=out_specs, check_vma=False
    )
```

```python
import functools

import jax
import jax.numpy as jnp
from jax import lax
from jax.experimental import pallas as pl
from jax.experimental.pallas import tpu as pltpu
from jax.sharding import PartitionSpec as P

MESH = pl.DeviceIdType.MESH
VMEM = 63 * 1024 * 1024
PARTS = 4
HALVES = 2


def contract(left, right):
    return lax.dot_general(
        left, right, (((1,), (1,)), ((), ())), preferred_element_type=jnp.float32
    )


def kernel(
    n_blk,
    n_feat,
    q_hbm,
    g_hbm,
    store_hbm,
    ids_hbm,
    mask_hbm,
    out_ref,
    ids_ref,
    mask_ref,
    q_all,
    gram,
    stored,
    e_all,
    p_send,
    p_recv,
    cond,
    local_sem,
    a_send,
    a_recv,
    e_send,
    e_recv,
    b_send,
    b_recv,
    c_send,
    c_recv,
):
    z = lax.axis_index("blk")
    f = lax.axis_index("feat")
    half = z // 2
    order = [z, z + 1 - 2 * half, 2 - 2 * z + 5 * half, 3 - 3 * half]
    first, second, far = order[1], order[2], order[3]
    end = 3 * half
    between = (z - 1) * (z - 2) == 0
    sibling = f + 1 - 2 * (f % 2)
    across = (f + 2) % 4

    load_q = pltpu.make_async_copy(q_hbm, q_all.at[z], local_sem.at[0])
    load_g = pltpu.make_async_copy(g_hbm, gram, local_sem.at[1])
    load_s = pltpu.make_async_copy(store_hbm, stored, local_sem.at[2])
    load_ids = pltpu.make_async_copy(ids_hbm, ids_ref, local_sem.at[3])
    load_mask = pltpu.make_async_copy(mask_hbm, mask_ref, local_sem.at[4])

    def send(src, dst, send_sem, recv_sem, target):
        return pltpu.make_async_remote_copy(
            src_ref=src,
            dst_ref=dst,
            send_sem=send_sem,
            recv_sem=recv_sem,
            device_id=target,
            device_id_type=MESH,
        )

    barrier = pltpu.get_barrier_semaphore()
    for d in range(1, n_blk):
        pl.semaphore_signal(
            barrier, inc=1, device_id={"blk": (z + d) % n_blk}, device_id_type=MESH
        )
    for d in range(1, n_feat):
        pl.semaphore_signal(
            barrier, inc=1, device_id={"feat": (f + d) % n_feat}, device_id_type=MESH
        )
    load_q.start()
    load_g.start()
    load_ids.start()
    load_s.start()
    load_mask.start()

    def a_copy(j, target, slot, i, src=None):
        size = q_hbm.shape[0] // HALVES
        rows = pl.ds(i * size, size)
        return send(
            q_all.at[j, rows] if src is None else src.at[rows],
            q_all.at[j, rows],
            a_send.at[slot, i],
            a_recv.at[j, i],
            {"blk": target},
        )

    def hand_on(s):
        @pl.when(between)
        def _():
            for i in range(HALVES):
                a_copy(order[s], z, 0, i).wait_recv()
                a_copy(order[s], end, 2 + s // 2, i).start()

    def b_copy(j, src, target):
        return send(
            p_send.at[j, target],
            p_recv.at[j, src],
            b_send.at[j, target],
            b_recv.at[j, src],
            {"feat": target},
        )

    def c_copy(c, j, target, slot):
        return send(
            cond.at[c, j],
            cond.at[c, j],
            c_send.at[j, slot],
            c_recv.at[c, j],
            {"blk": target},
        )

    def e_copy(src, slot, i, target):
        size = e_all.shape[1] // PARTS
        part = e_all.at[src, pl.ds(i * size, size)]
        return send(
            part, part, e_send.at[slot, i], e_recv.at[src, i], {"feat": target}
        )

    def push_e(i):
        if i < PARTS:
            e_copy(f, 0, i, across).start()
            e_copy(f, 1, i, sibling).start()

    def hand_over(i):
        e_copy(across, 2, i, f).wait_recv()
        e_copy(across, 2, i, sibling).start()

    def multiply(s):
        j = order[s]
        if s == 2:
            for i in range(HALVES):
                a_copy(j, z, 0, i).wait_recv()
        elif s > 0:

            @pl.when(jnp.logical_not(between))
            def _():
                for i in range(HALVES):
                    a_copy(j, z, 0, i).wait_recv()

        value = jnp.dot(q_all[j], gram[...], preferred_element_type=jnp.float32)
        rows = value.shape[0] // n_feat
        p_send[j] = value.astype(jnp.bfloat16).reshape(n_feat, rows, value.shape[1])

    def spread(s):
        for d in range(1, n_feat):
            b_copy(order[s], f, (f + d) % n_feat).start()

    def finish(s):
        j = order[s]
        total = p_send[j, f].astype(jnp.float32)
        for d in range(1, n_feat):
            src = (f + d) % n_feat
            b_copy(j, src, f).wait_recv()
            total = total + p_recv[j, src].astype(jnp.float32)
        cond[z, j] = total.astype(jnp.bfloat16)
        for t in (3, 2, 1):
            c_copy(z, j, order[t], t - 1).start()

    pl.semaphore_wait(barrier, n_blk + n_feat - 2)
    for i in range(HALVES):
        a_copy(z, first, 0, i, q_hbm).start()
    for i in range(HALVES):
        a_copy(z, second, 1, i, q_hbm).start()

    load_q.wait()
    load_g.wait()
    multiply(0)
    spread(0)
    load_ids.wait()
    load_s.wait()
    held = stored.shape[0]
    examples = ids_ref.shape[1]
    pick = jnp.where(
        lax.broadcasted_iota(jnp.int32, (held, examples), 0) == ids_ref[...], 1.0, 0.0
    ).astype(jnp.bfloat16)
    e_all[f] = lax.dot_general(
        pick, stored[...], (((0,), (0,)), ((), ())), preferred_element_type=jnp.float32
    ).astype(jnp.bfloat16)
    push_e(0)
    hand_on(1)
    multiply(1)
    spread(1)
    push_e(1)
    finish(0)
    multiply(2)
    spread(2)
    push_e(2)
    hand_on(3)
    finish(1)
    hand_over(0)
    multiply(3)
    spread(3)
    push_e(3)
    hand_over(1)
    finish(2)
    hand_over(2)
    finish(3)
    hand_over(3)
    for i in range(PARTS):
        e_copy(sibling, 1, i, f).wait_recv()
        e_copy((sibling + 2) % 4, 1, i, f).wait_recv()

    total = None
    for s in range(n_blk):
        c = order[s]
        if s > 0:
            for j in range(n_blk):
                c_copy(c, j, z, 0).wait_recv()
        rows = cond.shape[1] * cond.shape[2]
        value = contract(cond[c].reshape(rows, cond.shape[3]), e_all[c])
        total = value if total is None else total + value
    load_mask.wait()
    total = total.reshape(out_ref.shape)
    for j in range(n_blk):
        out_ref[j] = total[j] * mask_ref[0, j].astype(jnp.float32)

    for j in range(n_blk):
        for d in range(1, n_feat):
            b_copy(j, f, (f + d) % n_feat).wait_send()
        for t in range(1, n_blk):
            c_copy(z, j, order[t], t - 1).wait_send()
    for i in range(HALVES):
        a_copy(z, first, 0, i).wait_send()
        a_copy(z, second, 1, i).wait_send()

    @pl.when(between)
    def _():
        for i in range(HALVES):
            a_copy(z, end, 2, i).wait_send()
            a_copy(z, end, 3, i).wait_send()

    for slot in range(3):
        for i in range(PARTS):
            e_copy(f, slot, i, sibling).wait_send()


def fused(n_blk, n_feat, queries, inv_gram, store, ids, mask):
    qdev, width = queries.shape
    edev = ids.shape[1]
    rows = qdev // n_feat
    dma = pltpu.SemaphoreType.DMA
    any_spec = pl.BlockSpec(memory_space=pl.ANY)
    vmem_spec = pl.BlockSpec(memory_space=pltpu.VMEM)
    return pl.pallas_call(
        functools.partial(kernel, n_blk, n_feat),
        out_shape=jax.ShapeDtypeStruct((n_blk, rows, edev), jnp.float32),
        in_specs=[any_spec] * 5,
        out_specs=vmem_spec,
        scratch_shapes=[
            pltpu.VMEM(ids.shape, jnp.int32),
            pltpu.SMEM(mask.shape, jnp.int32),
            pltpu.VMEM((n_blk, qdev, width), jnp.bfloat16),
            pltpu.VMEM(inv_gram.shape, jnp.bfloat16),
            pltpu.VMEM(store.shape, jnp.bfloat16),
            pltpu.VMEM((n_feat, edev, width), jnp.bfloat16),
            pltpu.VMEM((n_blk, n_feat, rows, inv_gram.shape[1]), jnp.bfloat16),
            pltpu.VMEM((n_blk, n_feat, rows, inv_gram.shape[1]), jnp.bfloat16),
            pltpu.VMEM((n_blk, n_blk, rows, inv_gram.shape[1]), jnp.bfloat16),
            dma((5,)),
            dma((4, HALVES)),
            dma((n_blk, HALVES)),
            dma((3, PARTS)),
            dma((n_feat, PARTS)),
            dma((n_blk, n_feat)),
            dma((n_blk, n_feat)),
            dma((n_blk, n_blk)),
            dma((n_blk, n_blk)),
        ],
        compiler_params=pltpu.CompilerParams(
            collective_id=0, has_side_effects=True, vmem_limit_bytes=VMEM
        ),
    )(queries, inv_gram, store, ids, mask)


def plain(n_blk, n_feat, queries, inv_gram, store, ids, mask):
    gathered = lax.all_gather(queries, "blk", axis=0, tiled=True)
    partial_value = jnp.dot(gathered, inv_gram, preferred_element_type=jnp.float32)
    rows = queries.shape[0] // n_feat
    spread = partial_value.astype(jnp.bfloat16).reshape(n_blk, n_feat, rows, -1)
    precond = lax.psum_scatter(spread, "feat", scatter_dimension=1, tiled=True)
    precond = lax.all_gather(
        precond.reshape(n_blk * rows, -1), "blk", axis=1, tiled=True
    )
    examples = lax.all_gather(
        jnp.take(store, ids[0], axis=0), "feat", axis=1, tiled=True
    )
    raw = contract(precond, examples).reshape(n_blk, rows, -1)
    return raw * mask[0][:, None, None].astype(jnp.float32)


def per_device(queries, inv_gram, store, example_ids, example_weights, domain_mask):
    n_blk, n_feat = lax.axis_size("blk"), lax.axis_size("feat")
    lines = n_blk == 4 and n_feat == 4
    aligned = queries.shape[0] % (16 * n_feat) == 0 and queries.shape[1] % 128 == 0
    same = queries.shape[1] == inv_gram.shape[1]
    score = fused if lines and aligned and same else plain
    ids, mask = example_ids[None, :], domain_mask.reshape(1, n_blk)
    raw = score(n_blk, n_feat, queries, inv_gram, store, ids, mask)
    return raw * example_weights[None, None, :]


def solution(mesh):
    in_specs = (
        P(("grp", "blk"), "feat"),
        P("feat", "blk"),
        P(("grp", "blk"), "feat"),
        P(("grp", "blk")),
        P(("grp", "blk")),
        P("grp", "blk"),
    )
    out_specs = P(None, ("grp", "feat"), "blk")
    return jax.shard_map(
        per_device, mesh=mesh, in_specs=in_specs, out_specs=out_specs, check_vma=False
    )
```

```python
import functools

import jax
import jax.numpy as jnp
from jax import lax
from jax.experimental import pallas as pl
from jax.experimental.pallas import tpu as pltpu
from jax.sharding import PartitionSpec as P

MESH = pl.DeviceIdType.MESH
VMEM = 63 * 1024 * 1024
PARTS = 4
HALVES = 2


def contract(left, right):
    return lax.dot_general(
        left, right, (((1,), (1,)), ((), ())), preferred_element_type=jnp.float32
    )


def kernel(
    n_blk,
    n_feat,
    q_hbm,
    g_hbm,
    store_hbm,
    ids_hbm,
    mask_hbm,
    out_ref,
    ids_ref,
    mask_ref,
    q_all,
    gram,
    stored,
    e_all,
    p_send,
    p_recv,
    cond,
    local_sem,
    a_send,
    a_recv,
    e_send,
    e_recv,
    b_send,
    b_recv,
    c_send,
    c_recv,
):
    z = lax.axis_index("blk")
    f = lax.axis_index("feat")
    half = z // 2
    order = [z, z + 1 - 2 * half, 2 - 2 * z + 5 * half, 3 - 3 * half]
    first, second, far = order[1], order[2], order[3]
    end = 3 * half
    between = (z - 1) * (z - 2) == 0
    sibling = f + 1 - 2 * (f % 2)
    across = (f + 2) % 4

    load_q = pltpu.make_async_copy(q_hbm, q_all.at[z], local_sem.at[0])
    load_g = pltpu.make_async_copy(g_hbm, gram, local_sem.at[1])
    load_s = pltpu.make_async_copy(store_hbm, stored, local_sem.at[2])
    load_ids = pltpu.make_async_copy(ids_hbm, ids_ref, local_sem.at[3])
    load_mask = pltpu.make_async_copy(mask_hbm, mask_ref, local_sem.at[4])

    def send(src, dst, send_sem, recv_sem, target):
        return pltpu.make_async_remote_copy(
            src_ref=src,
            dst_ref=dst,
            send_sem=send_sem,
            recv_sem=recv_sem,
            device_id=target,
            device_id_type=MESH,
        )

    barrier = pltpu.get_barrier_semaphore()
    for d in range(1, n_blk):
        pl.semaphore_signal(
            barrier, inc=1, device_id={"blk": (z + d) % n_blk}, device_id_type=MESH
        )
    for d in range(1, n_feat):
        pl.semaphore_signal(
            barrier, inc=1, device_id={"feat": (f + d) % n_feat}, device_id_type=MESH
        )
    load_q.start()
    load_g.start()
    load_ids.start()
    load_s.start()
    load_mask.start()

    def a_copy(j, target, slot, i, src=None):
        size = q_hbm.shape[0] // HALVES
        rows = pl.ds(i * size, size)
        return send(
            q_all.at[j, rows] if src is None else src.at[rows],
            q_all.at[j, rows],
            a_send.at[slot, i],
            a_recv.at[j, i],
            {"blk": target},
        )

    def hand_on(s):
        @pl.when(between)
        def _():
            for i in range(HALVES):
                a_copy(order[s], z, 0, i).wait_recv()
                a_copy(order[s], end, 2 + s // 2, i).start()

    def b_copy(j, src, target):
        return send(
            p_send.at[j, target],
            p_recv.at[j, src],
            b_send.at[j, target],
            b_recv.at[j, src],
            {"feat": target},
        )

    def c_copy(c, j, target, slot):
        return send(
            cond.at[c, j],
            cond.at[c, j],
            c_send.at[j, slot],
            c_recv.at[c, j],
            {"blk": target},
        )

    def e_copy(src, slot, i, target):
        size = e_all.shape[1] // PARTS
        part = e_all.at[src, pl.ds(i * size, size)]
        return send(
            part, part, e_send.at[slot, i], e_recv.at[src, i], {"feat": target}
        )

    def push_e(i):
        if i < PARTS:
            e_copy(f, 0, i, across).start()
            e_copy(f, 1, i, sibling).start()

    def hand_over(i):
        e_copy(across, 2, i, f).wait_recv()
        e_copy(across, 2, i, sibling).start()

    def multiply(s):
        j = order[s]
        if s == 2:
            for i in range(HALVES):
                a_copy(j, z, 0, i).wait_recv()
        elif s > 0:

            @pl.when(jnp.logical_not(between))
            def _():
                for i in range(HALVES):
                    a_copy(j, z, 0, i).wait_recv()

        value = jnp.dot(q_all[j], gram[...], preferred_element_type=jnp.float32)
        rows = value.shape[0] // n_feat
        p_send[j] = value.astype(jnp.bfloat16).reshape(n_feat, rows, value.shape[1])

    def spread(s):
        for d in range(1, n_feat):
            b_copy(order[s], f, (f + d) % n_feat).start()

    def finish(s):
        j = order[s]
        total = p_send[j, f].astype(jnp.float32)
        for d in range(1, n_feat):
            src = (f + d) % n_feat
            b_copy(j, src, f).wait_recv()
            total = total + p_recv[j, src].astype(jnp.float32)
        cond[z, j] = total.astype(jnp.bfloat16)
        for t in (3, 2, 1):
            c_copy(z, j, order[t], t - 1).start()

    pl.semaphore_wait(barrier, n_blk + n_feat - 2)
    for i in range(HALVES):
        a_copy(z, first, 0, i, q_hbm).start()
    for i in range(HALVES):
        a_copy(z, second, 1, i, q_hbm).start()

    load_q.wait()
    load_g.wait()
    multiply(0)
    spread(0)
    load_ids.wait()
    load_s.wait()
    held = stored.shape[0]
    examples = ids_ref.shape[1]
    pick = jnp.where(
        lax.broadcasted_iota(jnp.int32, (held, examples), 0) == ids_ref[...], 1.0, 0.0
    ).astype(jnp.bfloat16)
    e_all[f] = lax.dot_general(
        pick, stored[...], (((0,), (0,)), ((), ())), preferred_element_type=jnp.float32
    ).astype(jnp.bfloat16)
    push_e(0)
    hand_on(1)
    multiply(1)
    spread(1)
    push_e(1)
    finish(0)
    multiply(2)
    spread(2)
    push_e(2)
    hand_on(3)
    finish(1)
    hand_over(0)
    multiply(3)
    spread(3)
    push_e(3)
    hand_over(1)
    finish(2)
    hand_over(2)
    finish(3)
    hand_over(3)
    total = None
    for s, c in enumerate((f, sibling, across, (sibling + 2) % 4)):
        if s % 2 == 1:
            for i in range(PARTS):
                e_copy(c, 1, i, f).wait_recv()

        @pl.when(c != z)
        def _():
            for j in range(n_blk):
                c_copy(c, j, z, 0).wait_recv()

        rows = cond.shape[1] * cond.shape[2]
        value = contract(cond[c].reshape(rows, cond.shape[3]), e_all[c])
        total = value if total is None else total + value
    load_mask.wait()
    total = total.reshape(out_ref.shape)
    for j in range(n_blk):
        out_ref[j] = total[j] * mask_ref[0, j].astype(jnp.float32)

    for j in range(n_blk):
        for d in range(1, n_feat):
            b_copy(j, f, (f + d) % n_feat).wait_send()
        for t in range(1, n_blk):
            c_copy(z, j, order[t], t - 1).wait_send()
    for i in range(HALVES):
        a_copy(z, first, 0, i).wait_send()
        a_copy(z, second, 1, i).wait_send()

    @pl.when(between)
    def _():
        for i in range(HALVES):
            a_copy(z, end, 2, i).wait_send()
            a_copy(z, end, 3, i).wait_send()

    for slot in range(3):
        for i in range(PARTS):
            e_copy(f, slot, i, sibling).wait_send()


def fused(n_blk, n_feat, queries, inv_gram, store, ids, mask):
    qdev, width = queries.shape
    edev = ids.shape[1]
    rows = qdev // n_feat
    dma = pltpu.SemaphoreType.DMA
    any_spec = pl.BlockSpec(memory_space=pl.ANY)
    vmem_spec = pl.BlockSpec(memory_space=pltpu.VMEM)
    return pl.pallas_call(
        functools.partial(kernel, n_blk, n_feat),
        out_shape=jax.ShapeDtypeStruct((n_blk, rows, edev), jnp.float32),
        in_specs=[any_spec] * 5,
        out_specs=vmem_spec,
        scratch_shapes=[
            pltpu.VMEM(ids.shape, jnp.int32),
            pltpu.SMEM(mask.shape, jnp.int32),
            pltpu.VMEM((n_blk, qdev, width), jnp.bfloat16),
            pltpu.VMEM(inv_gram.shape, jnp.bfloat16),
            pltpu.VMEM(store.shape, jnp.bfloat16),
            pltpu.VMEM((n_feat, edev, width), jnp.bfloat16),
            pltpu.VMEM((n_blk, n_feat, rows, inv_gram.shape[1]), jnp.bfloat16),
            pltpu.VMEM((n_blk, n_feat, rows, inv_gram.shape[1]), jnp.bfloat16),
            pltpu.VMEM((n_blk, n_blk, rows, inv_gram.shape[1]), jnp.bfloat16),
            dma((5,)),
            dma((4, HALVES)),
            dma((n_blk, HALVES)),
            dma((3, PARTS)),
            dma((n_feat, PARTS)),
            dma((n_blk, n_feat)),
            dma((n_blk, n_feat)),
            dma((n_blk, n_blk)),
            dma((n_blk, n_blk)),
        ],
        compiler_params=pltpu.CompilerParams(
            collective_id=0, has_side_effects=True, vmem_limit_bytes=VMEM
        ),
    )(queries, inv_gram, store, ids, mask)


def plain(n_blk, n_feat, queries, inv_gram, store, ids, mask):
    gathered = lax.all_gather(queries, "blk", axis=0, tiled=True)
    partial_value = jnp.dot(gathered, inv_gram, preferred_element_type=jnp.float32)
    rows = queries.shape[0] // n_feat
    spread = partial_value.astype(jnp.bfloat16).reshape(n_blk, n_feat, rows, -1)
    precond = lax.psum_scatter(spread, "feat", scatter_dimension=1, tiled=True)
    precond = lax.all_gather(
        precond.reshape(n_blk * rows, -1), "blk", axis=1, tiled=True
    )
    examples = lax.all_gather(
        jnp.take(store, ids[0], axis=0), "feat", axis=1, tiled=True
    )
    raw = contract(precond, examples).reshape(n_blk, rows, -1)
    return raw * mask[0][:, None, None].astype(jnp.float32)


def per_device(queries, inv_gram, store, example_ids, example_weights, domain_mask):
    n_blk, n_feat = lax.axis_size("blk"), lax.axis_size("feat")
    lines = n_blk == 4 and n_feat == 4
    aligned = queries.shape[0] % (16 * n_feat) == 0 and queries.shape[1] % 128 == 0
    same = queries.shape[1] == inv_gram.shape[1]
    score = fused if lines and aligned and same else plain
    ids, mask = example_ids[None, :], domain_mask.reshape(1, n_blk)
    raw = score(n_blk, n_feat, queries, inv_gram, store, ids, mask)
    return raw * example_weights[None, None, :]


def solution(mesh):
    in_specs = (
        P(("grp", "blk"), "feat"),
        P("feat", "blk"),
        P(("grp", "blk"), "feat"),
        P(("grp", "blk")),
        P(("grp", "blk")),
        P("grp", "blk"),
    )
    out_specs = P(None, ("grp", "feat"), "blk")
    return jax.shard_map(
        per_device, mesh=mesh, in_specs=in_specs, out_specs=out_specs, check_vma=False
    )
```
